32 devices in a mesh: snap: 4 (over y, core), gx: 4 (over z), gy: 2 (over x).
Axes of the slice: x: 2, y: 2, z: 4, core: 2. Of those that a mesh axis runs over, the one named last changes fastest.
Arguments:
- displacements: float32 [64, 3, 16, 256], P('snap', None, 'gx', 'gy')
- forces: float32 [64, 3, 16, 256], P('snap', None, 'gx', 'gy')
- neighbours: int32 [8, 16, 256], P(None, 'gx', 'gy'), may hold values 0 or 1
- species: int32 [16, 256], P('gx', 'gy'), may hold values from 0 to 2
- block_of: int32 [16, 256], P('gx', 'gy'), may hold values from 0 to 3, as said below
- precond: float32 [32, 3, 24, 24], P(('gx', 'gy')), may hold values from -0.1 to 0.8, as said below
- vectors: float32 [256, 3, 16, 256], P('snap', None, 'gx', 'gy'), may hold values from -6 to 6
Outputs:
- constants: float32 [32, 3, 24, 3], P(('gx', 'gy'))
- chebyshev: float32 [256, 3, 16, 256], P('snap', None, 'gx', 'gy')
The draws below stay inside these ranges and needn't reach their ends.
Inputs may be any that keep to these rules, and one draw needn't show every extreme that they name: `block_of`: on each device's 4 x 128 atoms, every block index holds exactly 128 atoms. `precond`: each matrix has its diagonal between 0.4 and 0.8 and small off-diagonal entries.
All inputs are finite; a program needn't handle non-finite values. No bound on the sum of `neighbours` on one device may be relied on, other than what follows from the above.
Results may differ from the reference program's by a relative error of at most 0.00011.
Values sent between devices are 32-bit elements; how exact they have to be, the bound alone decides.
A program may use at most 64 MiB of HBM per device.

```python
import jax
import jax.numpy as jnp
from jax import lax

AX = 4
AY = 128
AB = 128
NSPEC = 3
NOFF = 8
P_SIZE = 24
BLK_DEV = 4
NBLK = 32
GXA = 16
GYA = 256
SNAPS = 64
NV = 256


def joint_fields(key):
    base = jax.random.fold_in(key, 11)
    key_disp, key_stiff, key_noise = jax.random.split(base, 3)
    shape = (SNAPS, 3, GXA, GYA)
    moves = jax.random.normal(key_disp, shape, jnp.float32)
    stiff = jnp.exp(jax.random.uniform(key_stiff, (1, 3, GXA, GYA), jnp.float32, -0.7, 0.7))
    noise = jax.random.normal(key_noise, shape, jnp.float32)
    return (moves, -stiff * moves + 0.3 * noise)


def draw_displacements(key, part):
    return joint_fields(key)[0]


def draw_forces(key, part):
    return joint_fields(key)[1]


def draw_block_of(key, part):
    count_x = GXA // AX
    count_y = GYA // AY
    keys = jax.random.split(jax.random.fold_in(key, 23), count_x * count_y)
    perms = jax.vmap(lambda single: jax.random.permutation(single, AX * AY))(keys)
    blocks = (perms // AB).astype(jnp.int32).reshape(count_x, count_y, AX, AY)
    return blocks.transpose(0, 2, 1, 3).reshape(GXA, GYA)


def draw_precond(key, part):
    key_diag, key_off = jax.random.split(jax.random.fold_in(key, 37), 2)
    diag = jax.random.uniform(key_diag, (NBLK, NSPEC, P_SIZE), jnp.float32, 0.4, 0.8)
    off = jax.random.uniform(key_off, (NBLK, NSPEC, P_SIZE, P_SIZE), jnp.float32, -1.0, 1.0) * 0.1
    eye = jnp.eye(P_SIZE, dtype=jnp.float32)
    return off * (1.0 - eye) + eye * diag[..., None]


def touch_ends(values, stream_key, low, top_value):
    extent = values.shape
    spot = [jax.random.randint(jax.random.fold_in(stream_key, axis), (), 0, extent[axis]) for axis in range(len(extent))]
    values = values.at[tuple(spot)].set(low)
    longest = extent.index(max(extent))
    spot[longest] = (spot[longest] + 1) % extent[longest]
    return values.at[tuple(spot)].set(top_value)


def shard_levels(stream_key, shape, pieces, low, largest):
    factor_of, own = 1.0, jax.random.fold_in(stream_key, 6)
    for position, shards_of in pieces:
        heights = jnp.exp(jax.random.uniform(jax.random.fold_in(own, position), (shards_of,), jnp.float32, low / len(pieces), largest / len(pieces)))
        factor_of = factor_of * jnp.repeat(heights, shape[position] // shards_of).reshape([-1 if axis == position else 1 for axis in range(len(shape))])
    return factor_of


def gaussian(rng, shape, width, most, cuts=(), kind=jnp.bfloat16):
    level = shard_levels(rng, shape, cuts, -0.22, 0.18) if cuts else 1.0
    drawn = jax.random.normal(rng, shape, jnp.float32) * width * level
    return jnp.minimum(jnp.maximum(drawn, -most), most).astype(kind)


def setup_inputs(seed: int = 0) -> dict:
    splits = jax.random.split(jax.random.key(seed), 8)
    return {
        "displacements": draw_displacements(jax.random.fold_in(splits[7], 71), 0),
        "forces": draw_forces(jax.random.fold_in(splits[7], 71), 0),
        "neighbours": touch_ends((jax.random.randint(splits[2], (NOFF, GXA, GYA), 0, 4) < 3).astype(jnp.int32), jax.random.fold_in(splits[2], 1), 0, 1),
        "species": touch_ends(jax.random.randint(splits[3], (GXA, GYA), 0, NSPEC), jax.random.fold_in(splits[3], 1), 0, NSPEC - 1).astype(jnp.int32),
        "block_of": draw_block_of(jax.random.fold_in(splits[7], 71), 0),
        "precond": draw_precond(jax.random.fold_in(splits[7], 71), 0),
        "vectors": gaussian(splits[6], (NV, 3, GXA, GYA), 1.0, 6.0, ((0, 4), (2, 4), (3, 2)), jnp.float32),
    }


offsets = ((-1, -1), (-1, 0), (-1, 1), (0, -1), (0, 1), (1, -1), (1, 0), (1, 1))


def moved_field(field, step_x, step_y):
    return jnp.roll(field, (-step_x, -step_y), axis=(2, 3))


def apply_operator(field, weights):
    result = jnp.zeros_like(field)
    for index, (step_x, step_y) in enumerate(offsets):
        differ = moved_field(field, step_x, step_y) - field
        result = result - jnp.sum(differ[:, :, None] * weights[index][None], axis=1)
    return result


def refine(precond, gram, rhs):
    high = lax.Precision.HIGHEST
    first = jnp.einsum('gpq,gqa->gpa', precond, rhs, precision=high)
    remain = rhs - jnp.einsum('gpq,gqa->gpa', gram, first, precision=high)
    return first + jnp.einsum('gpq,gqa->gpa', precond, remain, precision=high)


def reference(displacements, forces, neighbours, species, block_of, precond, vectors):
    high = lax.Precision.HIGHEST
    mask = neighbours.astype(jnp.float32)
    parts = []
    for index, (step_x, step_y) in enumerate(offsets):
        parts.append((moved_field(displacements, step_x, step_y) - displacements) * mask[index][None, None])
    feats = jnp.stack(parts, 1).reshape(SNAPS, P_SIZE, GXA * GYA)
    loads = forces.reshape(SNAPS, 3, GXA * GYA)
    rows_idx = jnp.arange(GXA, dtype=jnp.int32)[:, None]
    cols_idx = jnp.arange(GYA, dtype=jnp.int32)[None, :]
    device_id = (rows_idx // AX) * (GYA // AY) + cols_idx // AY
    group = ((device_id * BLK_DEV + block_of) * NSPEC + species).reshape(GXA * GYA).astype(jnp.int32)
    n_groups = NBLK * NSPEC
    pair = jnp.einsum('spi,sqi->ipq', feats, feats, precision=high).reshape(GXA * GYA, P_SIZE * P_SIZE)
    cross = jnp.einsum('spi,sai->ipa', feats, loads, precision=high).reshape(GXA * GYA, P_SIZE * 3)
    scale = 1.0 / (SNAPS * AB)
    gram = jax.ops.segment_sum(pair, group, num_segments=n_groups).reshape(n_groups, P_SIZE, P_SIZE) * scale
    rhs = jax.ops.segment_sum(cross, group, num_segments=n_groups).reshape(n_groups, P_SIZE, 3) * scale
    theta = refine(precond.reshape(n_groups, P_SIZE, P_SIZE), gram, rhs)
    per_atom = theta.reshape(n_groups, P_SIZE * 3)[group]
    weights = per_atom.T.reshape(NOFF, 3, 3, GXA, GYA) * mask[:, None, None]
    first_term = apply_operator(vectors, weights)
    chebyshev = 2.0 * apply_operator(first_term, weights) - vectors
    return theta.reshape(NBLK, NSPEC, P_SIZE, 3), chebyshev
```

```python
import functools

import jax
import jax.numpy as jnp
import numpy as np
from jax import lax
from jax.experimental import pallas as pl
from jax.experimental.pallas import tpu as pltpu
from jax.sharding import PartitionSpec as P

AB = 128
NSPEC = 3
GP = 16
WIDTH = 24
PAIRS = [(p, q) for p in range(WIDTH) for q in range(p, WIDTH)]
NPAIR = len(PAIRS)
ENTRIES = 384
PARTS = 2
MESH = pl.DeviceIdType.MESH

offsets = ((-1, -1), (-1, 0), (-1, 1), (0, -1), (0, 1), (1, -1), (1, 0), (1, 1))


def expansion():
    table = np.zeros((608, ENTRIES), np.float32)
    for index, (p, q) in enumerate(PAIRS):
        table[p * WIDTH + q, index] = 1.0
        table[q * WIDTH + p, index] = 1.0
    for p in range(WIDTH):
        for a in range(3):
            table[WIDTH * WIDTH + p, NPAIR + 3 * p + a] = 1.0
    return table


def split(value, parts):
    out = []
    for _ in range(parts):
        piece = value.astype(jnp.bfloat16)
        out.append(piece)
        value = value - piece.astype(jnp.float32)
    return out


def dot_nt(left, right):
    return lax.dot_general(left, right, (((1,), (1,)), ((), ())), preferred_element_type=jnp.float32)


def dot_nn(left, right):
    return lax.dot_general(left, right, (((1,), (0,)), ((), ())), preferred_element_type=jnp.float32)


def kernel(
    n_snap, n_gx, n_gy, n_dev, v_dev, scale,
    disp, forc, neigh, spec, blk, pre, table, vec,
    theta_out, out,
    ed, ev, ef, pk, pleft, pright, ce, pf, fleft, fright, cf,
    de, ms, prs, tall, ws, wc,
    bar_rows_s, bar_rows_r, pk_s, pk_r, t_s, t_r, f_s, f_r,
):
    me = lax.axis_index("snap")
    gx = lax.axis_index("gx")
    gy = lax.axis_index("gy")
    up = lax.rem(gx + n_gx - 1, n_gx)
    down = lax.rem(gx + 1, n_gx)
    left = lax.rem(gy + n_gy - 1, n_gy)
    right = lax.rem(gy + 1, n_gy)
    sides = (left, right) if n_gy > 2 else (right,)
    peers = [lax.rem(me + k, n_snap) for k in range(1, n_snap)]

    barrier = pltpu.get_barrier_semaphore()
    around = [(x, gy) for x in (up, down)] + [(x, y) for y in sides for x in (up, gx, down)]
    for x, y in around:
        pl.semaphore_signal(barrier, inc=1, device_id=(me, x, y), device_id_type=MESH)
    for peer in peers:
        pl.semaphore_signal(barrier, inc=1, device_id=(peer, gx, gy), device_id_type=MESH)

    lane = lax.broadcasted_iota(jnp.int32, (8, 128), 1)
    first_lane = lane == 0
    last_lane = lane == 127
    even = lane % 2 == 0
    v_chunks = v_dev // 8
    d_chunks = n_dev // 8

    def pack_into(current, value, index):
        place = 2 * index
        return jnp.where((lane == place) | (lane == place + 1), pltpu.roll(value, place + 1, 1), current)

    def row_copies(field, at, send, recv):
        return [
            pltpu.make_async_remote_copy(
                src_ref=field.at[pl.ds(source, 3), at], dst_ref=field.at[pl.ds(target, 3), at],
                send_sem=send.at[k], recv_sem=recv.at[k], device_id=(me, x, gy), device_id_type=MESH)
            for k, (source, target, x) in enumerate(((12, 0, down), (3, 15, up)))
        ]

    def column_copies(packed, to_left, to_right, send, recv, first):
        made = []
        for side, (y, target) in enumerate(((right, to_left), (left, to_right))):
            for k, (source, place, size, x) in enumerate(((0, 3, 12, gx), (9, 0, 3, down), (0, 15, 3, up))):
                number = first + side * 3 + k
                made.append(pltpu.make_async_remote_copy(
                    src_ref=packed.at[pl.ds(source, size)], dst_ref=target.at[pl.ds(place, size)],
                    send_sem=send.at[number], recv_sem=recv.at[number], device_id=(me, x, y), device_id_type=MESH))
        return made

    def join_columns(from_left, from_right, target):
        for row in range(18):
            target[row] = jnp.where(even, pltpu.roll(from_right[row], 127, 1), pltpu.roll(from_left[row], 1, 1))

    for x in range(4):
        for b in range(3):
            row = x * 3 + b
            packed = jnp.zeros((8, 128), jnp.float32)
            for c in range(d_chunks):
                value = disp[pl.ds(c * 96 + b * 4 + x, 8, stride=12), :]
                ed[row + 3, pl.ds(c * 8, 8), :] = value
                packed = pack_into(packed, value, v_chunks + c)
            for c in range(v_chunks):
                value = vec[pl.ds(c * 96 + b * 4 + x, 8, stride=12), :]
                ev[row + 3, pl.ds(c * 8, 8), :] = value
                packed = pack_into(packed, value, c)
            pk[row] = packed

    pl.semaphore_wait(barrier, len(around) + len(peers))
    d_rows = row_copies(ed, pl.ds(0, n_dev), bar_rows_s.at[0], bar_rows_r.at[0])
    cols = column_copies(pk, pleft, pright, pk_s, pk_r, 0)
    v_rows = row_copies(ev, pl.ds(0, v_dev), bar_rows_s.at[1], bar_rows_r.at[1])
    for copy in d_rows + cols + v_rows:
        copy.start()

    for o in range(8):
        for x in range(4):
            mask = neigh[pl.ds(o * 4 + x, 1), :].astype(jnp.float32)
            for b in range(3):
                ms[x, pl.ds(3 * o + b, 1), :] = mask
    prs[pl.ds(372 * 8, 12 * 8), :] = jnp.zeros((12 * 8, 128), jnp.float32)
    group = blk[...] * NSPEC + spec[...]
    sub = lax.broadcasted_iota(jnp.int32, (GP * 3, 128), 0) % GP

    for copy in d_rows + cols:
        copy.wait_recv()
    join_columns(pleft, pright, ce)

    for row in range(18):
        for c in range(d_chunks):
            value = ed[row, pl.ds(c * 8, 8), :]
            rim = pltpu.roll(ce[row], 128 - (2 * (v_chunks + c) + 1), 1)
            de[0, row, pl.ds(c * 8, 8), :] = jnp.where(first_lane, rim, pltpu.roll(value, 1, 1))
            de[1, row, pl.ds(c * 8, 8), :] = value
            de[2, row, pl.ds(c * 8, 8), :] = jnp.where(last_lane, rim, pltpu.roll(value, 127, 1))

    total = jnp.zeros((GP, ENTRIES), jnp.float32)
    for x in range(4):
        feats = []
        for o, (dx, dy) in enumerate(offsets):
            for b in range(3):
                differ = de[dy + 1, (x + 1 + dx) * 3 + b] - de[1, (x + 1) * 3 + b]
                feats.append(differ * ms[x, pl.ds(3 * o + b, 1), :])
        loads = [forc[pl.ds(a * 4 + x, n_dev, stride=12), :] for a in range(3)]

        def fold(product):
            return sum(product[c * 8:(c + 1) * 8] for c in range(d_chunks))

        for index, (p, q) in enumerate(PAIRS):
            prs[pl.ds(index * 8, 8), :] = fold(feats[p] * feats[q])
        for p in range(WIDTH):
            for a in range(3):
                prs[pl.ds((NPAIR + 3 * p + a) * 8, 8), :] = fold(feats[p] * loads[a])
        summed = prs[pl.ds(0, ENTRIES, stride=8), :]
        for k in range(1, 8):
            summed = summed + prs[pl.ds(k, ENTRIES, stride=8), :]
        hot = (sub[:GP] == group[x:x + 1, :]).astype(jnp.float32).astype(jnp.bfloat16)
        for piece in split(summed, 2):
            total = total + dot_nt(hot, piece)

    tall[me] = total
    t_copies = []
    for k, peer in enumerate(peers):
        copy = pltpu.make_async_remote_copy(
            src_ref=tall.at[me], dst_ref=tall.at[me], send_sem=t_s.at[k], recv_sem=t_r.at[me],
            device_id=(peer, gx, gy), device_id_type=MESH)
        copy.start()
        t_copies.append(copy)
    for k, peer in enumerate(peers):
        pltpu.make_async_remote_copy(
            src_ref=tall.at[me], dst_ref=tall.at[peer], send_sem=t_s.at[k], recv_sem=t_r.at[peer],
            device_id=(peer, gx, gy), device_id_type=MESH).wait_recv()
    total = tall[0]
    for k in range(1, n_snap):
        total = total + tall[k]
    total = total * scale

    wide = jnp.concatenate([total, total, total], axis=0)
    column = lax.broadcasted_iota(jnp.int32, (GP * 3, ENTRIES), 1)
    comp = lax.broadcasted_iota(jnp.int32, (GP * 3, ENTRIES), 0) // GP
    wide = jnp.where((column < NPAIR) | (lax.rem(column, 3) == comp), wide, 0.0)
    full = sum(dot_nt(table[...], piece) for piece in split(wide, 3))
    gram = full[: WIDTH * WIDTH].reshape(WIDTH, WIDTH, GP * 3)
    rhs = full[WIDTH * WIDTH: WIDTH * WIDTH + WIDTH]
    inverse = pre[...].reshape(WIDTH, WIDTH, GP * 3)
    first = jnp.sum(inverse * rhs[None], axis=1)
    remain = rhs - jnp.sum(gram * first[None], axis=1)
    theta = first + jnp.sum(inverse * remain[None], axis=1)
    theta_out[...] = theta

    held = lax.broadcasted_iota(jnp.int32, (WIDTH, GP * 3), 1) // GP
    stacked = jnp.concatenate([jnp.where(held == a, theta, 0.0) for a in range(3)], axis=0)
    pieces = split(stacked, 3)
    for x in range(4):
        hot = (sub == group[x:x + 1, :]).astype(jnp.float32).astype(jnp.bfloat16)
        values = sum(dot_nn(piece, hot) for piece in pieces)
        mask = ms[x]
        ws[x] = values * jnp.concatenate([mask, mask, mask], axis=0)
        for a in range(3):
            for b in range(3):
                wc[x, pl.ds(a * 3 + b, 1), :] = jnp.sum(
                    ws[x, pl.ds(a * WIDTH + b, 8, stride=3), :], axis=0, keepdims=True)

    def stencil(field, rims, chunk, index, emit):
        start = pl.multiple_of(chunk * 8, 8)
        shift = 128 - (2 * index + 1)
        rows = []
        for row in range(18):
            value = field[row, pl.ds(start, 8), :]
            rim = pltpu.roll(rims[row], shift, 1)
            rows.append((
                jnp.where(first_lane, rim, pltpu.roll(value, 1, 1)),
                value,
                jnp.where(last_lane, rim, pltpu.roll(value, 127, 1)),
            ))
        for x in range(4):
            for a in range(3):
                acc = None
                for b in range(3):
                    term = wc[x, pl.ds(a * 3 + b, 1), :] * rows[(x + 1) * 3 + b][1]
                    acc = term if acc is None else acc + term
                for o, (dx, dy) in enumerate(offsets):
                    for b in range(3):
                        acc = acc - ws[x, pl.ds(a * WIDTH + 3 * o + b, 1), :] * rows[(x + 1 + dx) * 3 + b][dy + 1]
                emit(x, a, start, acc)

    for copy in v_rows:
        copy.wait_recv()

    per = v_chunks // PARTS
    f_copies = []
    for part in range(PARTS):
        pf[part] = jnp.zeros((12, 8, 128), jnp.float32)

        def first_step(k, carry, part=part):
            chunk = part * per + k

            def emit(x, a, start, acc):
                row = x * 3 + a
                ef[row + 3, pl.ds(start, 8), :] = acc
                pf[part, row] = pack_into(pf[part, row], acc, k)

            stencil(ev, ce, chunk, chunk, emit)
            return carry

        lax.fori_loop(0, per, first_step, 0)
        rows = row_copies(ef, pl.ds(part * per * 8, per * 8), f_s.at[part], f_r.at[part])
        columns = column_copies(pf.at[part], fleft.at[part], fright.at[part], f_s.at[part], f_r.at[part], 2)
        for copy in columns + rows:
            copy.start()
        f_copies.append(columns + rows)

    for part in range(PARTS):
        for copy in f_copies[part]:
            copy.wait_recv()
        join_columns(fleft.at[part], fright.at[part], cf)

        def second_step(k, carry, part=part):
            chunk = part * per + k

            def emit(x, a, start, acc):
                own = ev[(x + 1) * 3 + a, pl.ds(start, 8), :]
                out[pl.ds(chunk * 96 + a * 4 + x, 8, stride=12), :] = 2.0 * acc - own

            stencil(ef, cf, chunk, k, emit)
            return carry

        lax.fori_loop(0, per, second_step, 0)

    for copy in d_rows + cols + v_rows + t_copies + sum(f_copies, []):
        copy.wait_send()


def shards(displacements, forces, neighbours, species, block_of, precond, vectors):
    n_dev, _, rows, cols = displacements.shape
    v_dev = vectors.shape[0]
    n_snap, n_gx, n_gy = (lax.axis_size(name) for name in ("snap", "gx", "gy"))
    n_groups = precond.shape[0] * precond.shape[1]
    scale = 1.0 / (n_dev * n_snap * AB)
    inverse = precond.reshape(n_groups, WIDTH, WIDTH).transpose(1, 2, 0).reshape(WIDTH * WIDTH, n_groups)
    inverse = jnp.pad(inverse, ((0, 0), (0, GP - n_groups)))
    inverse = jnp.concatenate([inverse] * 3, axis=1)
    table = jnp.asarray(expansion(), jnp.bfloat16)
    vmem = pl.BlockSpec(memory_space=pltpu.VMEM)
    f32 = jnp.float32
    dma = pltpu.SemaphoreType.DMA
    theta, out = pl.pallas_call(
        functools.partial(kernel, n_snap, n_gx, n_gy, n_dev, v_dev, scale),
        out_shape=(
            jax.ShapeDtypeStruct((WIDTH, GP * 3), f32),
            jax.ShapeDtypeStruct((v_dev * 12, cols), f32),
        ),
        in_specs=[vmem] * 8,
        out_specs=(vmem, vmem),
        scratch_shapes=[
            pltpu.VMEM((18, n_dev, cols), f32),
            pltpu.VMEM((18, v_dev, cols), f32),
            pltpu.VMEM((18, v_dev, cols), f32),
            pltpu.VMEM((12, 8, cols), f32),
            pltpu.VMEM((18, 8, cols), f32),
            pltpu.VMEM((18, 8, cols), f32),
            pltpu.VMEM((18, 8, cols), f32),
            pltpu.VMEM((PARTS, 12, 8, cols), f32),
            pltpu.VMEM((PARTS, 18, 8, cols), f32),
            pltpu.VMEM((PARTS, 18, 8, cols), f32),
            pltpu.VMEM((18, 8, cols), f32),
            pltpu.VMEM((3, 18, n_dev, cols), f32),
            pltpu.VMEM((4, WIDTH, cols), f32),
            pltpu.VMEM((ENTRIES * 8, cols), f32),
            pltpu.VMEM((n_snap, GP, ENTRIES), f32),
            pltpu.VMEM((4, 3 * WIDTH, cols), f32),
            pltpu.VMEM((4, 16, cols), f32),
            dma((2, 2)), dma((2, 2)), dma((6,)), dma((6,)),
            dma((n_snap,)), dma((n_snap,)), dma((PARTS, 8)), dma((PARTS, 8)),
        ],
        compiler_params=pltpu.CompilerParams(
            collective_id=0, has_side_effects=True, vmem_limit_bytes=40 * 1024 * 1024),
        name="fit_and_apply",
    )(
        displacements.reshape(n_dev * 12, cols), forces.reshape(n_dev * 12, cols),
        neighbours.reshape(32, cols), species, block_of, inverse, table, vectors.reshape(v_dev * 12, cols),
    )
    theta = theta.reshape(WIDTH, 3, GP)[:, :, :n_groups].transpose(2, 0, 1)
    return (
        theta.reshape(precond.shape[0], precond.shape[1], WIDTH, 3),
        out.reshape(v_dev, 3, rows, cols),
    )


def solution(mesh):
    in_specs = (
        P("snap", None, "gx", "gy"),
        P("snap", None, "gx", "gy"),
        P(None, "gx", "gy"),
        P("gx", "gy"),
        P("gx", "gy"),
        P(("gx", "gy"), None, None, None),
        P("snap", None, "gx", "gy"),
    )
    out_specs = (P(("gx", "gy"), None, None, None), P("snap", None, "gx", "gy"))
    return jax.shard_map(shards, mesh=mesh, in_specs=in_specs, out_specs=out_specs, check_vma=False)
```

```python
import functools

import jax
import jax.numpy as jnp
import numpy as np
from jax import lax
from jax.experimental import pallas as pl
from jax.experimental.pallas import tpu as pltpu
from jax.sharding import PartitionSpec as P

AB = 128
NSPEC = 3
GP = 16
WIDTH = 24
PAIRS = [(p, q) for p in range(WIDTH) for q in range(p, WIDTH)]
NPAIR = len(PAIRS)
PLACES = {pair: index for index, pair in enumerate(PAIRS)}
ENTRIES = 384
PARTS = 4
MESH = pl.DeviceIdType.MESH

offsets = ((-1, -1), (-1, 0), (-1, 1), (0, -1), (0, 1), (1, -1), (1, 0), (1, 1))


def expansion():
    table = np.zeros((608, ENTRIES), np.float32)
    for index, (p, q) in enumerate(PAIRS):
        table[p * WIDTH + q, index] = 1.0
        table[q * WIDTH + p, index] = 1.0
    for p in range(WIDTH):
        for a in range(3):
            table[WIDTH * WIDTH + p, NPAIR + 3 * p + a] = 1.0
    return table


def split(value, parts):
    out = []
    for _ in range(parts):
        piece = value.astype(jnp.bfloat16)
        out.append(piece)
        value = value - piece.astype(jnp.float32)
    return out


def dot_nt(left, right):
    return lax.dot_general(left, right, (((1,), (1,)), ((), ())), preferred_element_type=jnp.float32)


def dot_nn(left, right):
    return lax.dot_general(left, right, (((1,), (0,)), ((), ())), preferred_element_type=jnp.float32)


def kernel(
    n_snap, n_gx, n_gy, n_dev, v_dev, scale,
    disp_in, forc_in, neigh_in, spec_in, blk_in, pre_in, table_in, vec_in,
    theta_out, out,
    disp, forc, neigh, spec, blk, raw, table, chosen, vec, load_sem, pre, feat,
    ed, ev, ef, pk, pleft, pright, ce, pf, fleft, fright, cf,
    de, ms, prs, tall, ws, wc,
    bar_rows_s, bar_rows_r, pk_s, pk_r, t_s, t_r, f_s, f_r,
):
    loads_in = [
        pltpu.make_async_copy(source, target, load_sem.at[k])
        for k, (source, target) in enumerate((
            (disp_in, disp), (vec_in, vec), (neigh_in, neigh), (spec_in, spec),
            (blk_in, blk), (forc_in, forc), (pre_in, raw), (table_in, table)))
    ]
    for copy in loads_in:
        copy.start()
    me = lax.axis_index("snap")
    gx = lax.axis_index("gx")
    gy = lax.axis_index("gy")
    up = lax.rem(gx + n_gx - 1, n_gx)
    down = lax.rem(gx + 1, n_gx)
    left = lax.rem(gy + n_gy - 1, n_gy)
    right = lax.rem(gy + 1, n_gy)
    sides = (left, right) if n_gy > 2 else (right,)
    peers = [lax.rem(me + k, n_snap) for k in range(1, n_snap)]

    barrier = pltpu.get_barrier_semaphore()
    around = [(x, gy) for x in (up, down)] + [(x, y) for y in sides for x in (up, gx, down)]
    for x, y in around:
        pl.semaphore_signal(barrier, inc=1, device_id=(me, x, y), device_id_type=MESH)
    for peer in peers:
        pl.semaphore_signal(barrier, inc=1, device_id=(peer, gx, gy), device_id_type=MESH)

    lane = lax.broadcasted_iota(jnp.int32, (8, 128), 1)
    first_lane = lane == 0
    last_lane = lane == 127
    even = lane % 2 == 0
    v_chunks = v_dev // 8
    d_chunks = n_dev // 8

    def pack_into(current, value, index):
        place = 2 * index
        return jnp.where((lane == place) | (lane == place + 1), pltpu.roll(value, place + 1, 1), current)

    def row_copies(field, at, send, recv):
        return [
            pltpu.make_async_remote_copy(
                src_ref=field.at[pl.ds(source, 3), at], dst_ref=field.at[pl.ds(target, 3), at],
                send_sem=send.at[k], recv_sem=recv.at[k], device_id=(me, x, gy), device_id_type=MESH)
            for k, (source, target, x) in enumerate(((12, 0, down), (3, 15, up)))
        ]

    def column_copies(packed, to_left, to_right, send, recv, first):
        made = []
        for side, (y, target) in enumerate(((right, to_left), (left, to_right))):
            for k, (source, place, size, x) in enumerate(((0, 3, 12, gx), (9, 0, 3, down), (0, 15, 3, up))):
                number = first + side * 3 + k
                made.append(pltpu.make_async_remote_copy(
                    src_ref=packed.at[pl.ds(source, size)], dst_ref=target.at[pl.ds(place, size)],
                    send_sem=send.at[number], recv_sem=recv.at[number], device_id=(me, x, y), device_id_type=MESH))
        return made

    def join_columns(from_left, from_right, target, rows=range(18)):
        for row in rows:
            target[row] = jnp.where(even, pltpu.roll(from_right[row], 127, 1), pltpu.roll(from_left[row], 1, 1))

    loads_in[0].wait()
    loads_in[1].wait()
    for x in range(4):
        for b in range(3):
            row = x * 3 + b
            packed = jnp.zeros((8, 128), jnp.float32)
            for c in range(d_chunks):
                value = disp[pl.ds(c * 96 + b * 4 + x, 8, stride=12), :]
                ed[row + 3, pl.ds(c * 8, 8), :] = value
                packed = pack_into(packed, value, v_chunks + c)
            for c in range(v_chunks):
                value = vec[pl.ds(c * 96 + b * 4 + x, 8, stride=12), :]
                ev[row + 3, pl.ds(c * 8, 8), :] = value
                packed = pack_into(packed, value, c)
            pk[row] = packed

    pl.semaphore_wait(barrier, len(around) + len(peers))
    d_rows = row_copies(ed, pl.ds(0, n_dev), bar_rows_s.at[0], bar_rows_r.at[0])
    cols = column_copies(pk, pleft, pright, pk_s, pk_r, 0)
    v_rows = row_copies(ev, pl.ds(0, v_dev), bar_rows_s.at[1], bar_rows_r.at[1])
    for copy in d_rows + cols + v_rows:
        copy.start()

    for copy in loads_in[2:]:
        copy.wait()
    for o in range(8):
        for x in range(4):
            mask = neigh[pl.ds(o * 4 + x, 1), :].astype(jnp.float32)
            for b in range(3):
                ms[x, pl.ds(3 * o + b, 1), :] = mask
    prs[pl.ds(372 * 8, 12 * 8), :] = jnp.zeros((12 * 8, 128), jnp.float32)
    group = blk[...] * NSPEC + spec[...]
    sub = lax.broadcasted_iota(jnp.int32, (GP * 3, 128), 0) % GP
    n_groups = raw.shape[0] // WIDTH
    matrices = raw[...].reshape(n_groups, WIDTH, WIDTH)
    blank = jnp.zeros((GP - n_groups, WIDTH), jnp.float32)
    for p in range(WIDTH):
        held_rows = jnp.concatenate([matrices[:, p, :], blank], axis=0)
        pre[p] = jnp.concatenate([held_rows] * 3, axis=0).T
    chosen[...] = table[...].astype(jnp.bfloat16)
    folds = n_dev * 4 // 8
    for a in range(3):
        for x in range(4):
            feat[WIDTH + a, pl.ds(x, n_dev, stride=4), :] = forc[pl.ds(a * 4 + x, n_dev, stride=12), :]

    for copy in d_rows + cols:
        copy.wait_recv()
    join_columns(pleft, pright, ce)

    for row in range(18):
        for c in range(d_chunks):
            value = ed[row, pl.ds(c * 8, 8), :]
            rim = pltpu.roll(ce[row], 128 - (2 * (v_chunks + c) + 1), 1)
            de[0, row, pl.ds(c * 8, 8), :] = jnp.where(first_lane, rim, pltpu.roll(value, 1, 1))
            de[1, row, pl.ds(c * 8, 8), :] = value
            de[2, row, pl.ds(c * 8, 8), :] = jnp.where(last_lane, rim, pltpu.roll(value, 127, 1))

    for o, (dx, dy) in enumerate(offsets):
        for b in range(3):
            for x in range(4):
                differ = de[dy + 1, (x + 1 + dx) * 3 + b] - de[1, (x + 1) * 3 + b]
                feat[3 * o + b, pl.ds(x, n_dev, stride=4), :] = differ * ms[x, pl.ds(3 * o + b, 1), :]
    for base in range(0, WIDTH, 4):
        kept = [[feat[p, pl.ds(8 * k, 8), :] for k in range(folds)] for p in range(base, base + 4)]
        for q in range(base, WIDTH + 3):
            other = [feat[q, pl.ds(8 * k, 8), :] for k in range(folds)]
            for p in range(base, min(base + 4, q + 1)):
                acc = kept[p - base][0] * other[0]
                for k in range(1, folds):
                    acc = acc + kept[p - base][k] * other[k]
                place = PLACES[p, q] if q < WIDTH else NPAIR + 3 * p + q - WIDTH
                prs[pl.ds(place * 8, 8), :] = acc
    total = jnp.zeros((GP, ENTRIES), jnp.float32)
    for x in range(4):
        summed = prs[pl.ds(x, ENTRIES, stride=8), :] + prs[pl.ds(x + 4, ENTRIES, stride=8), :]
        hot = (sub[:GP] == group[x:x + 1, :]).astype(jnp.float32).astype(jnp.bfloat16)
        for piece in split(summed, 2):
            total = total + dot_nt(hot, piece)

    tall[me] = total
    t_copies = []
    for k, peer in enumerate(peers):
        copy = pltpu.make_async_remote_copy(
            src_ref=tall.at[me], dst_ref=tall.at[me], send_sem=t_s.at[k], recv_sem=t_r.at[me],
            device_id=(peer, gx, gy), device_id_type=MESH)
        copy.start()
        t_copies.append(copy)
    for k, peer in enumerate(peers):
        pltpu.make_async_remote_copy(
            src_ref=tall.at[me], dst_ref=tall.at[peer], send_sem=t_s.at[k], recv_sem=t_r.at[peer],
            device_id=(peer, gx, gy), device_id_type=MESH).wait_recv()
    total = tall[0]
    for k in range(1, n_snap):
        total = total + tall[k]
    total = total * scale

    wide = jnp.concatenate([total, total, total], axis=0)
    column = lax.broadcasted_iota(jnp.int32, (GP * 3, ENTRIES), 1)
    comp = lax.broadcasted_iota(jnp.int32, (GP * 3, ENTRIES), 0) // GP
    wide = jnp.where((column < NPAIR) | (lax.rem(column, 3) == comp), wide, 0.0)
    full = sum(dot_nt(chosen[...], piece) for piece in split(wide, 3))
    gram = full[: WIDTH * WIDTH].reshape(WIDTH, WIDTH, GP * 3)
    rhs = full[WIDTH * WIDTH: WIDTH * WIDTH + WIDTH]
    inverse = pre[...]
    first = jnp.sum(inverse * rhs[None], axis=1)
    remain = rhs - jnp.sum(gram * first[None], axis=1)
    theta = first + jnp.sum(inverse * remain[None], axis=1)

    held = lax.broadcasted_iota(jnp.int32, (WIDTH, GP * 3), 1) // GP
    stacked = jnp.concatenate([jnp.where(held == a, theta, 0.0) for a in range(3)], axis=0)
    pieces = split(stacked, 3)
    for x in range(4):
        hot = (sub == group[x:x + 1, :]).astype(jnp.float32).astype(jnp.bfloat16)
        values = sum(dot_nn(piece, hot) for piece in pieces)
        mask = ms[x]
        ws[x] = values * jnp.concatenate([mask, mask, mask], axis=0)
        for a in range(3):
            for b in range(3):
                wc[x, pl.ds(a * 3 + b, 1), :] = jnp.sum(
                    ws[x, pl.ds(a * WIDTH + b, 8, stride=3), :], axis=0, keepdims=True)

    def stencil(field, rims, chunk, index, emit, picked):
        start = pl.multiple_of(chunk * 8, 8)
        shift = 128 - (2 * index + 1)
        rows = {}
        for row in range(picked[0] * 3, (picked[-1] + 3) * 3):
            value = field[row, pl.ds(start, 8), :]
            rim = pltpu.roll(rims[row], shift, 1)
            rows[row] = (
                jnp.where(first_lane, rim, pltpu.roll(value, 1, 1)),
                value,
                jnp.where(last_lane, rim, pltpu.roll(value, 127, 1)),
            )
        for x in picked:
            for a in range(3):
                acc = None
                for b in range(3):
                    term = wc[x, pl.ds(a * 3 + b, 1), :] * rows[(x + 1) * 3 + b][1]
                    acc = term if acc is None else acc + term
                for o, (dx, dy) in enumerate(offsets):
                    for b in range(3):
                        acc = acc - ws[x, pl.ds(a * WIDTH + 3 * o + b, 1), :] * rows[(x + 1 + dx) * 3 + b][dy + 1]
                emit(x, a, start, acc)

    for copy in v_rows:
        copy.wait_recv()

    per = v_chunks // PARTS
    f_copies = []
    for part in range(PARTS):
        pf[part] = jnp.zeros((12, 8, 128), jnp.float32)

        def first_step(k, carry, part=part):
            chunk = part * per + k

            def emit(x, a, start, acc):
                row = x * 3 + a
                ef[row + 3, pl.ds(start, 8), :] = acc
                pf[part, row] = pack_into(pf[part, row], acc, k)

            stencil(ev, ce, chunk, chunk, emit, (0, 1, 2, 3))
            return carry

        lax.fori_loop(0, per, first_step, 0)
        rows = row_copies(ef, pl.ds(part * per * 8, per * 8), f_s.at[part], f_r.at[part])
        columns = column_copies(pf.at[part], fleft.at[part], fright.at[part], f_s.at[part], f_r.at[part], 2)
        for copy in columns + rows:
            copy.start()
        f_copies.append(columns + rows)

    turned = theta.T
    n_blocks = theta_out.shape[2]
    for kind in range(NSPEC):
        for a in range(3):
            for block in range(n_blocks):
                row = a * GP + block * NSPEC + kind
                theta_out[kind, a, pl.ds(block, 1), :] = turned[row:row + 1, :]

    def second(part, picked):
        def second_step(k, carry):
            chunk = part * per + k

            def emit(x, a, start, acc):
                own = ev[(x + 1) * 3 + a, pl.ds(start, 8), :]
                out[pl.ds(chunk * 96 + a * 4 + x, 8, stride=12), :] = 2.0 * acc - own

            stencil(ef, cf.at[part], chunk, k, emit, picked)
            return carry

        lax.fori_loop(0, per, second_step, 0)

    for part in range(PARTS):
        f_copies[part][0].wait_recv()
        f_copies[part][3].wait_recv()
        join_columns(fleft.at[part], fright.at[part], cf.at[part], range(3, 15))
        second(part, (1, 2))
    for part in range(PARTS):
        for k in (1, 2, 4, 5, 6, 7):
            f_copies[part][k].wait_recv()
        join_columns(fleft.at[part], fright.at[part], cf.at[part], (0, 1, 2, 15, 16, 17))
        second(part, (0, 3))

    for copy in d_rows + cols + v_rows + t_copies + sum(f_copies, []):
        copy.wait_send()


def shards(displacements, forces, neighbours, species, block_of, precond, vectors):
    n_dev, _, rows, cols = displacements.shape
    v_dev = vectors.shape[0]
    n_snap, n_gx, n_gy = (lax.axis_size(name) for name in ("snap", "gx", "gy"))
    n_groups = precond.shape[0] * precond.shape[1]
    scale = 1.0 / (n_dev * n_snap * AB)
    table = jnp.asarray(expansion())
    vmem = pl.BlockSpec(memory_space=pltpu.VMEM)
    hbm = pl.BlockSpec(memory_space=pltpu.HBM)
    f32 = jnp.float32
    dma = pltpu.SemaphoreType.DMA
    theta, out = pl.pallas_call(
        functools.partial(kernel, n_snap, n_gx, n_gy, n_dev, v_dev, scale),
        out_shape=(
            jax.ShapeDtypeStruct((NSPEC, 3, precond.shape[0], WIDTH), f32),
            jax.ShapeDtypeStruct((v_dev * 12, cols), f32),
        ),
        in_specs=[hbm] * 8,
        out_specs=(vmem, vmem),
        scratch_shapes=[
            pltpu.VMEM((n_dev * 12, cols), f32),
            pltpu.VMEM((n_dev * 12, cols), f32),
            pltpu.VMEM((32, cols), jnp.int32),
            pltpu.VMEM((rows, cols), jnp.int32),
            pltpu.VMEM((rows, cols), jnp.int32),
            pltpu.VMEM((n_groups * WIDTH, WIDTH), f32),
            pltpu.VMEM(table.shape, f32),
            pltpu.VMEM(table.shape, jnp.bfloat16),
            pltpu.VMEM((v_dev * 12, cols), f32),
            dma((8,)),
            pltpu.VMEM((WIDTH, WIDTH, GP * 3), f32),
            pltpu.VMEM((WIDTH + 3, n_dev * 4, cols), f32),
            pltpu.VMEM((18, n_dev, cols), f32),
            pltpu.VMEM((18, v_dev, cols), f32),
            pltpu.VMEM((18, v_dev, cols), f32),
            pltpu.VMEM((12, 8, cols), f32),
            pltpu.VMEM((18, 8, cols), f32),
            pltpu.VMEM((18, 8, cols), f32),
            pltpu.VMEM((18, 8, cols), f32),
            pltpu.VMEM((PARTS, 12, 8, cols), f32),
            pltpu.VMEM((PARTS, 18, 8, cols), f32),
            pltpu.VMEM((PARTS, 18, 8, cols), f32),
            pltpu.VMEM((PARTS, 18, 8, cols), f32),
            pltpu.VMEM((3, 18, n_dev, cols), f32),
            pltpu.VMEM((4, WIDTH, cols), f32),
            pltpu.VMEM((ENTRIES * 8, cols), f32),
            pltpu.VMEM((n_snap, GP, ENTRIES), f32),
            pltpu.VMEM((4, 3 * WIDTH, cols), f32),
            pltpu.VMEM((4, 16, cols), f32),
            dma((2, 2)), dma((2, 2)), dma((6,)), dma((6,)),
            dma((n_snap,)), dma((n_snap,)), dma((PARTS, 8)), dma((PARTS, 8)),
        ],
        compiler_params=pltpu.CompilerParams(
            collective_id=0, has_side_effects=True, vmem_limit_bytes=62 * 1024 * 1024),
        name="fit_and_apply",
    )(
        displacements.reshape(n_dev * 12, cols), forces.reshape(n_dev * 12, cols),
        neighbours.reshape(32, cols), species, block_of, precond.reshape(n_groups * WIDTH, WIDTH), table, vectors.reshape(v_dev * 12, cols),
    )
    return (
        theta.transpose(2, 0, 3, 1),
        out.reshape(v_dev, 3, rows, cols),
    )


def solution(mesh):
    in_specs = (
        P("snap", None, "gx", "gy"),
        P("snap", None, "gx", "gy"),
        P(None, "gx", "gy"),
        P("gx", "gy"),
        P("gx", "gy"),
        P(("gx", "gy"), None, None, None),
        P("snap", None, "gx", "gy"),
    )
    out_specs = (P(("gx", "gy"), None, None, None), P("snap", None, "gx", "gy"))
    return jax.shard_map(shards, mesh=mesh, in_specs=in_specs, out_specs=out_specs, check_vma=False)
```

```python
import functools

import jax
import jax.numpy as jnp
import numpy as np
from jax import lax
from jax.experimental import pallas as pl
from jax.experimental.pallas import tpu as pltpu
from jax.sharding import PartitionSpec as P

AB = 128
NSPEC = 3
GP = 16
WIDTH = 24
DIAGS = WIDTH // 2 + 1
STEP = DIAGS + 3
FORCE = WIDTH + DIAGS - 1
ENTRIES = 384
PARTS = 4
MESH = pl.DeviceIdType.MESH

offsets = ((-1, -1), (-1, 0), (-1, 1), (0, -1), (0, 1), (1, -1), (1, 0), (1, 1))


def expansion():
    table = np.zeros((608, ENTRIES), np.float32)
    for p in range(WIDTH):
        for d in range(DIAGS):
            q = (p + d) % WIDTH
            table[p * WIDTH + q, p * STEP + d] = 1.0
            if d < DIAGS - 1:
                table[q * WIDTH + p, p * STEP + d] = 1.0
        table[WIDTH * WIDTH + p, p * STEP + DIAGS: (p + 1) * STEP] = 1.0
    return table


def split(value, parts):
    out = []
    for _ in range(parts):
        piece = value.astype(jnp.bfloat16)
        out.append(piece)
        value = value - piece.astype(jnp.float32)
    return out


def dot_nt(left, right):
    return lax.dot_general(left, right, (((1,), (1,)), ((), ())), preferred_element_type=jnp.float32)


def dot_nn(left, right):
    return lax.dot_general(left, right, (((1,), (0,)), ((), ())), preferred_element_type=jnp.float32)


def kernel(
    n_snap, n_gx, n_gy, n_dev, v_dev, scale,
    disp_in, forc_in, neigh_in, spec_in, blk_in, pre_in, table_in, vec_in,
    theta_out, out,
    disp, forc, neigh, spec, blk, raw, table, chosen, vec, load_sem, pre, feat, grp, full, fit, half,
    ed, ev, ef, pk, pleft, pright, ce, pf, fleft, fright, cf,
    de, ms, prs, tall, ws, wc,
    bar_rows_s, bar_rows_r, pk_s, pk_r, t_s, t_r, f_s, f_r,
):
    loads_in = [
        pltpu.make_async_copy(source, target, load_sem.at[k])
        for k, (source, target) in enumerate((
            (disp_in, disp), (vec_in, vec), (neigh_in, neigh), (spec_in, spec),
            (blk_in, blk), (forc_in, forc), (pre_in, raw), (table_in, table)))
    ]
    for copy in loads_in:
        copy.start()
    me = lax.axis_index("snap")
    gx = lax.axis_index("gx")
    gy = lax.axis_index("gy")
    up = lax.rem(gx + n_gx - 1, n_gx)
    down = lax.rem(gx + 1, n_gx)
    left = lax.rem(gy + n_gy - 1, n_gy)
    right = lax.rem(gy + 1, n_gy)
    sides = (left, right) if n_gy > 2 else (right,)
    peers = [lax.rem(me + k, n_snap) for k in range(1, n_snap)]

    barrier = pltpu.get_barrier_semaphore()
    around = [(x, gy) for x in (up, down)] + [(x, y) for y in sides for x in (up, gx, down)]
    for x, y in around:
        pl.semaphore_signal(barrier, inc=1, device_id=(me, x, y), device_id_type=MESH)
    for peer in peers:
        pl.semaphore_signal(barrier, inc=1, device_id=(peer, gx, gy), device_id_type=MESH)

    lane = lax.broadcasted_iota(jnp.int32, (8, 128), 1)
    first_lane = lane == 0
    last_lane = lane == 127
    even = lane % 2 == 0
    v_chunks = v_dev // 8
    d_chunks = n_dev // 8

    def pack_into(current, value, index):
        place = 2 * index
        return jnp.where((lane == place) | (lane == place + 1), pltpu.roll(value, place + 1, 1), current)

    def row_copies(field, at, send, recv):
        return [
            pltpu.make_async_remote_copy(
                src_ref=field.at[pl.ds(source, 3), at], dst_ref=field.at[pl.ds(target, 3), at],
                send_sem=send.at[k], recv_sem=recv.at[k], device_id=(me, x, gy), device_id_type=MESH)
            for k, (source, target, x) in enumerate(((12, 0, down), (3, 15, up)))
        ]

    def column_copies(packed, to_left, to_right, send, recv, first):
        made = []
        for side, (y, target) in enumerate(((right, to_left), (left, to_right))):
            for k, (source, place, size, x) in enumerate(((0, 3, 12, gx), (9, 0, 3, down), (0, 15, 3, up))):
                number = first + side * 3 + k
                made.append(pltpu.make_async_remote_copy(
                    src_ref=packed.at[pl.ds(source, size)], dst_ref=target.at[pl.ds(place, size)],
                    send_sem=send.at[number], recv_sem=recv.at[number], device_id=(me, x, y), device_id_type=MESH))
        return made

    def join_columns(from_left, from_right, target, low=0, high=18):
        def join(row, carry):
            target[row] = jnp.where(even, pltpu.roll(from_right[row], 127, 1), pltpu.roll(from_left[row], 1, 1))
            return carry

        lax.fori_loop(low, high, join, 0, unroll=3)

    loads_in[0].wait()
    loads_in[1].wait()
    def stage(row, carry):
        place = lax.rem(row, 3) * 4 + row // 3
        packed = jnp.zeros((8, 128), jnp.float32)
        for c in range(d_chunks):
            value = disp[pl.ds(c * 96 + place, 8, stride=12), :]
            ed[row + 3, pl.ds(c * 8, 8), :] = value
            packed = pack_into(packed, value, v_chunks + c)
        for c in range(v_chunks):
            value = vec[pl.ds(c * 96 + place, 8, stride=12), :]
            ev[row + 3, pl.ds(c * 8, 8), :] = value
            packed = pack_into(packed, value, c)
        pk[row] = packed
        return carry

    lax.fori_loop(0, 12, stage, 0)

    pl.semaphore_wait(barrier, len(around) + len(peers))
    d_rows = row_copies(ed, pl.ds(0, n_dev), bar_rows_s.at[0], bar_rows_r.at[0])
    cols = column_copies(pk, pleft, pright, pk_s, pk_r, 0)
    v_rows = row_copies(ev, pl.ds(0, v_dev), bar_rows_s.at[1], bar_rows_r.at[1])
    for copy in d_rows + cols + v_rows:
        copy.start()

    for copy in loads_in[2:]:
        copy.wait()
    for o in range(8):
        for x in range(4):
            mask = neigh[pl.ds(o * 4 + x, 1), :].astype(jnp.float32)
            for b in range(3):
                ms[x, pl.ds(3 * o + b, 1), :] = mask
    grp[...] = blk[...] * NSPEC + spec[...]
    sub = lax.broadcasted_iota(jnp.int32, (GP * 3, 128), 0) % GP
    n_groups = raw.shape[0] // WIDTH
    blank = jnp.zeros((GP - n_groups, WIDTH), jnp.float32)

    def turn(p, carry):
        held_rows = jnp.concatenate([raw[pl.ds(p, n_groups, stride=WIDTH), :][:, :WIDTH], blank], axis=0)
        pre[p] = jnp.concatenate([held_rows] * 3, axis=0).T
        return carry

    lax.fori_loop(0, WIDTH, turn, 0, unroll=4)

    def choose(k, carry):
        chosen[pl.ds(k * 32, 32), :] = table[pl.ds(k * 32, 32), :].astype(jnp.bfloat16)
        return carry

    lax.fori_loop(0, 19, choose, 0)
    folds = n_dev * 4 // 8
    def place_forces(x, carry):
        for a in range(3):
            feat[FORCE + a, pl.ds(x, n_dev, stride=4), :] = forc[pl.ds(a * 4 + x, n_dev, stride=12), :]
        return carry

    lax.fori_loop(0, 4, place_forces, 0)

    for copy in d_rows + cols:
        copy.wait_recv()
    join_columns(pleft, pright, ce)

    def widen(row, carry):
        for c in range(d_chunks):
            value = ed[row, pl.ds(c * 8, 8), :]
            rim = pltpu.roll(ce[row], 128 - (2 * (v_chunks + c) + 1), 1)
            de[0, row, pl.ds(c * 8, 8), :] = jnp.where(first_lane, rim, pltpu.roll(value, 1, 1))
            de[1, row, pl.ds(c * 8, 8), :] = value
            de[2, row, pl.ds(c * 8, 8), :] = jnp.where(last_lane, rim, pltpu.roll(value, 127, 1))

        return carry

    lax.fori_loop(0, 18, widen, 0)

    def features(x, carry):
        for o, (dx, dy) in enumerate(offsets):
            for b in range(3):
                p = 3 * o + b
                differ = de[dy + 1, (x + 1 + dx) * 3 + b] - de[1, (x + 1) * 3 + b]
                value = differ * ms[x, pl.ds(p, 1), :]
                feat[p, pl.ds(x, n_dev, stride=4), :] = value
                if p < DIAGS - 1:
                    feat[WIDTH + p, pl.ds(x, n_dev, stride=4), :] = value
        return carry

    lax.fori_loop(0, 4, features, 0)

    def products(p, carry):
        kept = [feat[p, pl.ds(8 * k, 8), :] for k in range(folds)]
        for d in range(STEP):
            q = p + d if d < DIAGS else FORCE + d - DIAGS
            acc = kept[0] * feat[q, pl.ds(0, 8), :]
            for k in range(1, folds):
                acc = acc + kept[k] * feat[q, pl.ds(8 * k, 8), :]
            prs[pl.ds(pl.multiple_of((p * STEP + d) * 8, 8), 8), :] = acc
        return carry

    lax.fori_loop(0, WIDTH, products, 0)

    def regroup(x, total):
        summed = prs[pl.ds(x, ENTRIES, stride=8), :] + prs[pl.ds(x + 4, ENTRIES, stride=8), :]
        hot = (sub[:GP] == grp[pl.ds(x, 1), :]).astype(jnp.float32).astype(jnp.bfloat16)
        for piece in split(summed, 2):
            total = total + dot_nt(hot, piece)
        return total

    total = lax.fori_loop(0, 4, regroup, jnp.zeros((GP, ENTRIES), jnp.float32))

    tall[me] = total
    t_copies = []
    for k, peer in enumerate(peers):
        copy = pltpu.make_async_remote_copy(
            src_ref=tall.at[me], dst_ref=tall.at[me], send_sem=t_s.at[k], recv_sem=t_r.at[me],
            device_id=(peer, gx, gy), device_id_type=MESH)
        copy.start()
        t_copies.append(copy)
    for k, peer in enumerate(peers):
        pltpu.make_async_remote_copy(
            src_ref=tall.at[me], dst_ref=tall.at[peer], send_sem=t_s.at[k], recv_sem=t_r.at[peer],
            device_id=(peer, gx, gy), device_id_type=MESH).wait_recv()
    total = tall[0]
    for k in range(1, n_snap):
        total = total + tall[k]
    total = total * scale

    wide = jnp.concatenate([total, total, total], axis=0)
    column = lax.broadcasted_iota(jnp.int32, (GP * 3, ENTRIES), 1)
    comp = lax.broadcasted_iota(jnp.int32, (GP * 3, ENTRIES), 0) // GP
    kind_of = column % STEP
    wide = jnp.where((kind_of < DIAGS) | (kind_of - DIAGS == comp), wide, 0.0)
    wide_pieces = split(wide, 3)
    for block in range(2):
        part_of = pl.ds(block * 304, 304)
        full[part_of, :] = sum(dot_nt(chosen[part_of, :], piece) for piece in wide_pieces)
    rhs = full[pl.ds(WIDTH * WIDTH, WIDTH), :]

    def apply_to(rows_of, operand, target):
        def one(p, carry):
            target[pl.ds(p, 1), :] = jnp.sum(rows_of(p) * operand, axis=0, keepdims=True)
            return carry

        lax.fori_loop(0, WIDTH, one, 0, unroll=8)
        return target[...]

    first = apply_to(lambda p: pre[p], rhs, fit)
    remain = rhs - apply_to(lambda p: full[pl.ds(pl.multiple_of(p * WIDTH, 8), WIDTH), :], first, half)
    theta = first + apply_to(lambda p: pre[p], remain, fit)

    held = lax.broadcasted_iota(jnp.int32, (WIDTH, GP * 3), 1) // GP
    stacked = jnp.concatenate([jnp.where(held == a, theta, 0.0) for a in range(3)], axis=0)
    pieces = split(stacked, 3)
    def weigh(x, carry):
        hot = (sub == grp[pl.ds(x, 1), :]).astype(jnp.float32).astype(jnp.bfloat16)
        values = sum(dot_nn(piece, hot) for piece in pieces)
        mask = ms[x]
        ws[x] = values * jnp.concatenate([mask, mask, mask], axis=0)
        for a in range(3):
            for b in range(3):
                wc[x, pl.ds(a * 3 + b, 1), :] = jnp.sum(
                    ws[x, pl.ds(a * WIDTH + b, 8, stride=3), :], axis=0, keepdims=True)
        return carry

    lax.fori_loop(0, 4, weigh, 0)

    def stencil(field, rims, chunk, index, emit, picked):
        start = pl.multiple_of(chunk * 8, 8)
        shift = 128 - (2 * index + 1)
        rows = {}
        for row in range(picked[0] * 3, (picked[-1] + 3) * 3):
            value = field[row, pl.ds(start, 8), :]
            rim = pltpu.roll(rims[row], shift, 1)
            rows[row] = (
                jnp.where(first_lane, rim, pltpu.roll(value, 1, 1)),
                value,
                jnp.where(last_lane, rim, pltpu.roll(value, 127, 1)),
            )
        for x in picked:
            for a in range(3):
                acc = None
                for b in range(3):
                    term = wc[x, pl.ds(a * 3 + b, 1), :] * rows[(x + 1) * 3 + b][1]
                    acc = term if acc is None else acc + term
                for o, (dx, dy) in enumerate(offsets):
                    for b in range(3):
                        acc = acc - ws[x, pl.ds(a * WIDTH + 3 * o + b, 1), :] * rows[(x + 1 + dx) * 3 + b][dy + 1]
                emit(x, a, start, acc)

    for copy in v_rows:
        copy.wait_recv()

    per = v_chunks // PARTS
    pf[...] = jnp.zeros(pf.shape, jnp.float32)

    def sent(part):
        rows = row_copies(ef, pl.ds(pl.multiple_of(part * (per * 8), 8), per * 8), f_s.at[part], f_r.at[part])
        columns = column_copies(pf.at[part], fleft.at[part], fright.at[part], f_s.at[part], f_r.at[part], 2)
        return columns + rows

    def first_part(part, carry):
        def first_step(k, carry):
            chunk = part * per + k

            def emit(x, a, start, acc):
                row = x * 3 + a
                ef[row + 3, pl.ds(start, 8), :] = acc
                pf[part, row] = pack_into(pf[part, row], acc, k)

            stencil(ev, ce, chunk, chunk, emit, (0, 1, 2, 3))
            return carry

        lax.fori_loop(0, per, first_step, 0)
        for copy in sent(part):
            copy.start()
        return carry

    lax.fori_loop(0, PARTS, first_part, 0)

    turned = theta.T
    n_blocks = theta_out.shape[2]
    for kind in range(NSPEC):
        for a in range(3):
            for block in range(n_blocks):
                row = a * GP + block * NSPEC + kind
                theta_out[kind, a, pl.ds(block, 1), :] = turned[row:row + 1, :]

    def second(part, picked):
        def second_step(k, carry):
            chunk = part * per + k

            def emit(x, a, start, acc):
                own = ev[(x + 1) * 3 + a, pl.ds(start, 8), :]
                out[pl.ds(chunk * 96 + a * 4 + x, 8, stride=12), :] = 2.0 * acc - own

            stencil(ef, cf.at[part], chunk, k, emit, picked)
            return carry

        lax.fori_loop(0, per, second_step, 0)

    def inner(part, carry):
        copies = sent(part)
        copies[0].wait_recv()
        copies[3].wait_recv()
        join_columns(fleft.at[part], fright.at[part], cf.at[part], 3, 15)
        second(part, (1, 2))
        return carry

    def outer(part, carry):
        copies = sent(part)
        for k in (1, 2, 4, 5, 6, 7):
            copies[k].wait_recv()
        join_columns(fleft.at[part], fright.at[part], cf.at[part], 0, 3)
        join_columns(fleft.at[part], fright.at[part], cf.at[part], 15, 18)
        second(part, (0, 3))
        for copy in copies:
            copy.wait_send()
        return carry

    lax.fori_loop(0, PARTS, inner, 0)
    lax.fori_loop(0, PARTS, outer, 0)
    for copy in d_rows + cols + v_rows + t_copies:
        copy.wait_send()


def shards(displacements, forces, neighbours, species, block_of, precond, vectors):
    n_dev, _, rows, cols = displacements.shape
    v_dev = vectors.shape[0]
    n_snap, n_gx, n_gy = (lax.axis_size(name) for name in ("snap", "gx", "gy"))
    n_groups = precond.shape[0] * precond.shape[1]
    scale = 1.0 / (n_dev * n_snap * AB)
    table = jnp.asarray(expansion())
    vmem = pl.BlockSpec(memory_space=pltpu.VMEM)
    hbm = pl.BlockSpec(memory_space=pltpu.HBM)
    f32 = jnp.float32
    dma = pltpu.SemaphoreType.DMA
    theta, out = pl.pallas_call(
        functools.partial(kernel, n_snap, n_gx, n_gy, n_dev, v_dev, scale),
        out_shape=(
            jax.ShapeDtypeStruct((NSPEC, 3, precond.shape[0], WIDTH), f32),
            jax.ShapeDtypeStruct((v_dev * 12, cols), f32),
        ),
        in_specs=[hbm] * 8,
        out_specs=(vmem, vmem),
        scratch_shapes=[
            pltpu.VMEM((n_dev * 12, cols), f32),
            pltpu.VMEM((n_dev * 12, cols), f32),
            pltpu.VMEM((32, cols), jnp.int32),
            pltpu.VMEM((rows, cols), jnp.int32),
            pltpu.VMEM((rows, cols), jnp.int32),
            pltpu.VMEM((n_groups * WIDTH, WIDTH), f32),
            pltpu.VMEM(table.shape, f32),
            pltpu.VMEM(table.shape, jnp.bfloat16),
            pltpu.VMEM((v_dev * 12, cols), f32),
            dma((8,)),
            pltpu.VMEM((WIDTH, WIDTH, GP * 3), f32),
            pltpu.VMEM((FORCE + 3, n_dev * 4, cols), f32),
            pltpu.VMEM((4, cols), jnp.int32),
            pltpu.VMEM((608, GP * 3), f32),
            pltpu.VMEM((WIDTH, GP * 3), f32),
            pltpu.VMEM((WIDTH, GP * 3), f32),
            pltpu.VMEM((18, n_dev, cols), f32),
            pltpu.VMEM((18, v_dev, cols), f32),
            pltpu.VMEM((18, v_dev, cols), f32),
            pltpu.VMEM((12, 8, cols), f32),
            pltpu.VMEM((18, 8, cols), f32),
            pltpu.VMEM((18, 8, cols), f32),
            pltpu.VMEM((18, 8, cols), f32),
            pltpu.VMEM((PARTS, 12, 8, cols), f32),
            pltpu.VMEM((PARTS, 18, 8, cols), f32),
            pltpu.VMEM((PARTS, 18, 8, cols), f32),
            pltpu.VMEM((PARTS, 18, 8, cols), f32),
            pltpu.VMEM((3, 18, n_dev, cols), f32),
            pltpu.VMEM((4, WIDTH, cols), f32),
            pltpu.VMEM((ENTRIES * 8, cols), f32),
            pltpu.VMEM((n_snap, GP, ENTRIES), f32),
            pltpu.VMEM((4, 3 * WIDTH, cols), f32),
            pltpu.VMEM((4, 16, cols), f32),
            dma((2, 2)), dma((2, 2)), dma((6,)), dma((6,)),
            dma((n_snap,)), dma((n_snap,)), dma((PARTS, 8)), dma((PARTS, 8)),
        ],
        compiler_params=pltpu.CompilerParams(
            collective_id=0, has_side_effects=True, vmem_limit_bytes=62 * 1024 * 1024),
        name="fit_and_apply",
    )(
        displacements.reshape(n_dev * 12, cols), forces.reshape(n_dev * 12, cols),
        neighbours.reshape(32, cols), species, block_of, precond.reshape(n_groups * WIDTH, WIDTH), table, vectors.reshape(v_dev * 12, cols),
    )
    return (
        theta.transpose(2, 0, 3, 1),
        out.reshape(v_dev, 3, rows, cols),
    )


def solution(mesh):
    in_specs = (
        P("snap", None, "gx", "gy"),
        P("snap", None, "gx", "gy"),
        P(None, "gx", "gy"),
        P("gx", "gy"),
        P("gx", "gy"),
        P(("gx", "gy"), None, None, None),
        P("snap", None, "gx", "gy"),
    )
    out_specs = (P(("gx", "gy"), None, None, None), P("snap", None, "gx", "gy"))
    return jax.shard_map(shards, mesh=mesh, in_specs=in_specs, out_specs=out_specs, check_vma=False)
```
